32 devices in a mesh: sub: 4 (over z), tile: 8 (over y, x, core).
Axes of the slice: x: 2, y: 2, z: 4, core: 2. Of those that a mesh axis runs over, the one named last changes fastest.
Arguments:
- echoes: float32 [8, 32, 128], P('sub', 'tile'), may hold values from -6 to 6
- pulse_offset: float32 [8, 32], P('sub', 'tile'), may hold values from 0 to 1
- range_gates: int32 [8, 32, 64], P('sub', 'tile'), may hold values from 0 to 511
- visible: int32 [8, 64], P('sub', 'tile'), may hold values 0 or 1
Outputs:
- images: float32 [8, 64, 128, 256], P('sub', 'tile')
- peak: float32 [64, 128, 128], P('tile', 'sub')
The draws below stay inside these ranges and needn't reach their ends.
All inputs are finite; a program needn't handle non-finite values. No bound on the sum of `visible` on one device may be relied on, other than what follows from the above.
Results may differ from the reference program's by a relative error of at most 0.0037.
Values sent between devices are 32-bit elements; how exact they have to be, the bound alone decides.
A program may use at most 64 MiB of HBM per device.

```python
import math
import jax
import jax.numpy as jnp
from jax import lax

PULSE_H = 32
FREQS = 64
PIX = 128
GATES = 512
HALVES = 8
TILES = 64


def plant(drawn, key, least, high):
    shape = drawn.shape
    place = [jax.random.randint(jax.random.fold_in(key, axis), (), 0, shape[axis]) for axis in range(len(shape))]
    drawn = drawn.at[tuple(place)].set(least)
    longest = shape.index(max(shape))
    place[longest] = (place[longest] + 1) % shape[longest]
    return drawn.at[tuple(place)].set(high)


def block_scale(own_key, shape, split, least, high):
    def one(position, blocks):
        steps = jax.random.uniform(jax.random.fold_in(jax.random.fold_in(own_key, 6), position), (blocks,), jnp.float32, least / len(split), high / len(split))
        return jnp.repeat(jnp.exp(steps), shape[position] // blocks).reshape((-1,) + (1,) * (len(shape) - position - 1))

    level = one(*split[0])
    for cut in split[1:]:
        level = level * one(*cut)
    return level


def bell_draw(rng, dims, spread, reach, shards=(), held_as=jnp.bfloat16):
    factor_of = block_scale(rng, dims, shards, -0.22, 0.18) if shards else 1.0
    drawn = jax.random.normal(rng, dims, jnp.float32) * spread * factor_of
    return jnp.minimum(jnp.maximum(drawn, -reach), reach).astype(held_as)


def setup_inputs(seed: int = 0) -> dict:
    splits = jax.random.split(jax.random.key(seed), 5)
    return {
        "echoes": bell_draw(splits[0], (HALVES, PULSE_H, 2 * FREQS), 1.0, 6.0, ((0, 4), (1, 8)), jnp.float32),
        "pulse_offset": jnp.clip(1.0 * jax.random.uniform(splits[1], (HALVES, PULSE_H), jnp.float32) ** block_scale(splits[1], (HALVES, PULSE_H), ((0, 4), (1, 8)), -0.2, 0.2), 0.0, 1.0),
        "range_gates": plant(jax.random.randint(splits[2], (HALVES, PULSE_H, FREQS), 0, GATES), jax.random.fold_in(splits[2], 1), 0, GATES - 1).astype(jnp.int32),
        "visible": plant((jax.random.randint(splits[3], (HALVES, TILES), 0, 4) < 3).astype(jnp.int32), jax.random.fold_in(splits[3], 1), 0, 1),
    }


grid_cols = 16
two_pi = 2.0 * math.pi


def make_right(sine_wave):
    pixels = jnp.arange(PIX, dtype=jnp.float32)
    phase_grid = sine_wave[:, None] * pixels[None, :]
    real_part = jnp.cos(phase_grid).astype(jnp.bfloat16)
    imag_part = jnp.sin(phase_grid).astype(jnp.bfloat16)
    upper = jnp.concatenate([real_part, imag_part], axis=1)
    lower = jnp.concatenate([-imag_part, real_part], axis=1)
    return jnp.concatenate([upper, lower], axis=0)


def make_base(cosine_wave):
    pixels = jnp.arange(PIX, dtype=jnp.float32)
    base_phase = cosine_wave[None, :] * pixels[:, None]
    return jnp.cos(base_phase), jnp.sin(base_phase)


def make_left(echo_real, echo_imag, cosine_wave, sine_wave, base_cos, base_sin, tile_number, norm_scale):
    column = ((tile_number % grid_cols) * PIX - 8 * PIX).astype(jnp.float32)
    row_start = ((tile_number // grid_cols) * PIX - 4 * PIX).astype(jnp.float32)
    offset_phase = cosine_wave * column + sine_wave * row_start
    offset_cos = jnp.cos(offset_phase)
    offset_sin = jnp.sin(offset_phase)
    turned_real = norm_scale * (echo_real * offset_cos - echo_imag * offset_sin)
    turned_imag = norm_scale * (echo_real * offset_sin + echo_imag * offset_cos)
    real_part = turned_real[None, :] * base_cos - turned_imag[None, :] * base_sin
    imag_part = turned_real[None, :] * base_sin + turned_imag[None, :] * base_cos
    return jnp.concatenate([real_part, imag_part], axis=1).astype(jnp.bfloat16)


def half_image(fields):
    echo_half, offset_half, gates_half, shown_row, half_number = fields
    angle = two_pi * (half_number.astype(jnp.float32) + offset_half) / HALVES
    wave = 0.5 + gates_half.astype(jnp.float32) / GATES
    cosine_wave = (wave * jnp.cos(angle)[:, None]).reshape(-1)
    sine_wave = (wave * jnp.sin(angle)[:, None]).reshape(-1)
    echo_real = echo_half[:, :FREQS].reshape(-1)
    echo_imag = echo_half[:, FREQS:].reshape(-1)
    right_side = make_right(sine_wave)
    base_cos, base_sin = make_base(cosine_wave)
    norm_scale = (2.0 * PULSE_H * FREQS) ** -0.5

    def one_tile(tile_number):
        left_side = make_left(echo_real, echo_imag, cosine_wave, sine_wave, base_cos, base_sin, tile_number, norm_scale)
        return jnp.dot(left_side, right_side, preferred_element_type=jnp.float32)

    result = lax.map(one_tile, jnp.arange(TILES, dtype=jnp.int32))
    return result * shown_row.astype(jnp.float32)[:, None, None]


def reference(echoes, pulse_offset, range_gates, visible):
    halves = lax.map(half_image, (echoes, pulse_offset, range_gates, visible, jnp.arange(HALVES, dtype=jnp.int32)))
    images = halves + jnp.roll(halves, -1, axis=0)
    power_map = images[..., :PIX] ** 2 + images[..., PIX:] ** 2
    peak = jnp.max(power_map, axis=0)
    return images, peak
```

```python
import functools
import math

import jax
import jax.numpy as jnp
from jax import lax
from jax.experimental import pallas as pl
from jax.experimental.pallas import tpu as pltpu
from jax.sharding import PartitionSpec as P

PULSE_H = 32
FREQS = 64
PIX = 128
GATES = 512

grid_cols = 16
two_pi = 2.0 * math.pi

HALF_PI_A = 1.5703125
HALF_PI_B = 4.837512969970703e-4
HALF_PI_C = 7.549789948768648e-8


def sincos(phase):
    turns = jnp.floor(phase * (2.0 / math.pi) + 0.5)
    rest = phase - turns * HALF_PI_A
    rest = rest - turns * HALF_PI_B
    rest = rest - turns * HALF_PI_C
    quadrant = turns.astype(jnp.int32)
    square = rest * rest
    sine = -1.9515295891e-4 * square + 8.3321608736e-3
    sine = sine * square - 1.6666654611e-1
    sine = sine * square * rest + rest
    cosine = 2.443315711809948e-5 * square - 1.388731625493765e-3
    cosine = cosine * square + 4.166664568298827e-2
    cosine = cosine * square * square - 0.5 * square + 1.0
    odd = (quadrant & 1) == 1
    cos_out = jnp.where(odd, sine, cosine)
    sin_out = jnp.where(odd, cosine, sine)
    cos_out = jnp.where(((quadrant + 1) & 2) == 2, -cos_out, cos_out)
    sin_out = jnp.where((quadrant & 2) == 2, -sin_out, sin_out)
    return cos_out, sin_out


def powers(wave, start, rows):
    have = min(8, rows)
    steps = (lax.broadcasted_iota(jnp.int32, (have, wave.shape[1]), 0) + start).astype(jnp.float32)
    cos_rows, sin_rows = sincos(wave * steps)
    turn_cos, turn_sin = sincos(wave * float(have))
    while have < rows:
        next_cos = cos_rows * turn_cos - sin_rows * turn_sin
        next_sin = cos_rows * turn_sin + sin_rows * turn_cos
        cos_rows = jnp.concatenate([cos_rows, next_cos], axis=0)
        sin_rows = jnp.concatenate([sin_rows, next_sin], axis=0)
        turn_cos, turn_sin = turn_cos * turn_cos - turn_sin * turn_sin, 2.0 * turn_cos * turn_sin
        have *= 2
    return cos_rows, sin_rows


def image_kernel(sizes, shown_ref, pulses_ref, images_ref, peak_ref, left_ref, right_ref, acc_ref, prev_ref, own_first, own_prev):
    half_dev, sub_count, tile_count, tile_dev, own_rows, block = sizes
    half_total = half_dev * sub_count
    step = pl.program_id(0)
    sub = lax.axis_index("sub")
    first_tile = lax.axis_index("tile") * tile_dev
    half = lax.rem(sub * half_dev + step, half_total)
    source = lax.div(half, half_dev) * tile_count
    slot = lax.rem(half, half_dev)
    own_start = sub * own_rows
    norm_scale = (2.0 * PULSE_H * FREQS) ** (-0.5)

    def accumulate(rows, start):
        total = rows * tile_dev

        def chunk(d, carry):
            part = pulses_ref[source + d, slot]
            echo_real, echo_imag = part[0:1], part[1:2]
            cosine_wave, sine_wave = part[2:3], part[3:4]
            right_cos, right_sin = powers(sine_wave, 0, PIX)
            right_cos, right_sin = right_cos.astype(jnp.bfloat16), right_sin.astype(jnp.bfloat16)
            right_ref[:PIX, :block] = right_cos
            right_ref[:PIX, block:] = -right_sin
            right_ref[PIX:, :block] = right_sin
            right_ref[PIX:, block:] = right_cos
            base_cos, base_sin = powers(cosine_wave, start, rows)
            tiles = lax.broadcasted_iota(jnp.int32, (tile_dev, block), 0) + first_tile
            column = (lax.rem(tiles, grid_cols) * PIX - 8 * PIX).astype(jnp.float32)
            row_start = (lax.div(tiles, grid_cols) * PIX - 4 * PIX).astype(jnp.float32)
            offset_cos, offset_sin = sincos(cosine_wave * column + sine_wave * row_start)
            turned_real = norm_scale * (echo_real * offset_cos - echo_imag * offset_sin)
            turned_imag = norm_scale * (echo_real * offset_sin + echo_imag * offset_cos)
            pieces = []
            for i in range(tile_dev):
                real, imag = turned_real[i : i + 1], turned_imag[i : i + 1]
                left_real = real * base_cos - imag * base_sin
                left_imag = real * base_sin + imag * base_cos
                if rows % 16 == 0:
                    left_ref[i * rows : (i + 1) * rows, :block] = left_real.astype(jnp.bfloat16)
                    left_ref[i * rows : (i + 1) * rows, block:] = left_imag.astype(jnp.bfloat16)
                else:
                    pieces.append(jnp.concatenate([left_real, left_imag], axis=1))
            if pieces:
                left_ref[:total, :] = jnp.concatenate(pieces, axis=0).astype(jnp.bfloat16)
            term = lax.dot_general(
                left_ref[:total, :], right_ref[...], (((1,), (1,)), ((), ())),
                preferred_element_type=jnp.float32,
            )
            acc_ref[:total, :] += term
            return carry

        acc_ref[:total, :] = jnp.zeros((total, 2 * PIX), jnp.float32)
        lax.fori_loop(0, tile_count, chunk, 0)

    def add_power(i, own):
        power = own[:, :PIX] * own[:, :PIX] + own[:, PIX:] * own[:, PIX:]
        peak_ref[i] = jnp.maximum(peak_ref[i], power)

    @pl.when(step <= half_dev)
    def _():
        accumulate(PIX, 0)
        for i in range(tile_dev):
            shown = shown_ref[half, i].astype(jnp.float32)
            acc_ref[i * PIX : (i + 1) * PIX, :] = acc_ref[i * PIX : (i + 1) * PIX, :] * shown

        @pl.when(step == 0)
        def _():
            peak_ref[...] = jnp.zeros_like(peak_ref)
            for i in range(tile_dev):
                own_first[i] = acc_ref[pl.ds(pl.multiple_of(own_start + i * PIX, 8), own_rows), :]

        for i in range(tile_dev):
            own = acc_ref[pl.ds(pl.multiple_of(own_start + i * PIX, 8), own_rows), :]

            @pl.when(step > 0)
            def _():
                images_ref[0, i] = prev_ref[i * PIX : (i + 1) * PIX, :] + acc_ref[i * PIX : (i + 1) * PIX, :]
                add_power(i, own_prev[i] + own)

            prev_ref[i * PIX : (i + 1) * PIX, :] = acc_ref[i * PIX : (i + 1) * PIX, :]
            own_prev[i] = own

    @pl.when(step > half_dev)
    def _():
        accumulate(own_rows, own_start)
        for i in range(tile_dev):
            shown = shown_ref[half, i].astype(jnp.float32)
            own = acc_ref[i * own_rows : (i + 1) * own_rows, :] * shown
            add_power(i, own_prev[i] + own)
            own_prev[i] = own

    @pl.when(step == half_total - 1)
    def _():
        for i in range(tile_dev):
            if half_total > half_dev:
                add_power(i, own_prev[i] + own_first[i])


def on_device(echoes, pulse_offset, range_gates, visible):
    half_dev, pulse_dev, _ = echoes.shape
    tile_dev = visible.shape[1]
    sub_count = lax.axis_size("sub")
    tile_count = lax.axis_size("tile")
    half_total = half_dev * sub_count
    own_rows = PIX // sub_count
    block = pulse_dev * FREQS
    half_numbers = lax.axis_index("sub") * half_dev + jnp.arange(half_dev, dtype=jnp.int32)
    angles = two_pi * (half_numbers.astype(jnp.float32)[:, None] + pulse_offset) / half_total
    waves = 0.5 + range_gates.astype(jnp.float32) / GATES
    cosine_wave = waves * jnp.cos(angles)[:, :, None]
    sine_wave = waves * jnp.sin(angles)[:, :, None]
    mine = jnp.stack([echoes[:, :, :FREQS], echoes[:, :, FREQS:], cosine_wave, sine_wave], axis=1)
    mine = mine.reshape(half_dev, 4, block)
    pulses = lax.all_gather(mine, ("sub", "tile"), axis=0, tiled=False)
    shown = lax.all_gather(visible, "sub", axis=0, tiled=True)
    sizes = (half_dev, sub_count, tile_count, tile_dev, own_rows, block)
    images, peak = pl.pallas_call(
        functools.partial(image_kernel, sizes),
        grid=(half_total,),
        out_shape=(
            jax.ShapeDtypeStruct((half_dev, tile_dev, PIX, 2 * PIX), jnp.float32),
            jax.ShapeDtypeStruct((tile_dev, own_rows, PIX), jnp.float32),
        ),
        in_specs=[
            pl.BlockSpec(memory_space=pltpu.SMEM),
            pl.BlockSpec((sub_count * tile_count, half_dev, 4, block), lambda j: (0, 0, 0, 0)),
        ],
        out_specs=(
            pl.BlockSpec((1, tile_dev, PIX, 2 * PIX), lambda j: (jnp.clip(j - 1, 0, half_dev - 1), 0, 0, 0)),
            pl.BlockSpec((tile_dev, own_rows, PIX), lambda j: (0, 0, 0)),
        ),
        scratch_shapes=[
            pltpu.VMEM((tile_dev * PIX, 2 * block), jnp.bfloat16),
            pltpu.VMEM((2 * PIX, 2 * block), jnp.bfloat16),
            pltpu.VMEM((tile_dev * PIX, 2 * PIX), jnp.float32),
            pltpu.VMEM((tile_dev * PIX, 2 * PIX), jnp.float32),
            pltpu.VMEM((tile_dev, own_rows, 2 * PIX), jnp.float32),
            pltpu.VMEM((tile_dev, own_rows, 2 * PIX), jnp.float32),
        ],
        compiler_params=pltpu.CompilerParams(vmem_limit_bytes=40 * 2**20),
    )(shown, pulses)
    return images, peak


def solution(mesh):
    in_specs = (P("sub", "tile", None), P("sub", "tile"), P("sub", "tile", None), P("sub", "tile"))
    out_specs = (P("sub", "tile", None, None), P("tile", "sub", None))
    return jax.shard_map(
        on_device, mesh=mesh, in_specs=in_specs, out_specs=out_specs, check_vma=False
    )
```

```python
import functools
import math

import jax
import jax.numpy as jnp
from jax import lax
from jax.experimental import pallas as pl
from jax.experimental.pallas import tpu as pltpu
from jax.sharding import PartitionSpec as P

PULSE_H = 32
FREQS = 64
PIX = 128
GATES = 512

grid_cols = 16
two_pi = 2.0 * math.pi
MESH = pl.DeviceIdType.MESH

HALF_PI_A = 1.5703125
HALF_PI_B = 4.837512969970703e-4
HALF_PI_C = 7.549789948768648e-8


def sincos(phase):
    turns = jnp.floor(phase * (2.0 / math.pi) + 0.5)
    rest = phase - turns * HALF_PI_A
    rest = rest - turns * HALF_PI_B
    rest = rest - turns * HALF_PI_C
    quadrant = turns.astype(jnp.int32)
    square = rest * rest
    sine = -1.9515295891e-4 * square + 8.3321608736e-3
    sine = sine * square - 1.6666654611e-1
    sine = sine * square * rest + rest
    cosine = 2.443315711809948e-5 * square - 1.388731625493765e-3
    cosine = cosine * square + 4.166664568298827e-2
    cosine = cosine * square * square - 0.5 * square + 1.0
    odd = (quadrant & 1) == 1
    cos_out = jnp.where(odd, sine, cosine)
    sin_out = jnp.where(odd, cosine, sine)
    cos_out = jnp.where(((quadrant + 1) & 2) == 2, -cos_out, cos_out)
    sin_out = jnp.where((quadrant & 2) == 2, -sin_out, sin_out)
    return cos_out, sin_out


def powers(wave, start, rows):
    have = min(8, rows)
    steps = (lax.broadcasted_iota(jnp.int32, (have, wave.shape[1]), 0) + start).astype(jnp.float32)
    cos_rows, sin_rows = sincos(wave * steps)
    turn_cos, turn_sin = sincos(wave * float(have))
    while have < rows:
        next_cos = cos_rows * turn_cos - sin_rows * turn_sin
        next_sin = cos_rows * turn_sin + sin_rows * turn_cos
        cos_rows = jnp.concatenate([cos_rows, next_cos], axis=0)
        sin_rows = jnp.concatenate([sin_rows, next_sin], axis=0)
        turn_cos, turn_sin = turn_cos * turn_cos - turn_sin * turn_sin, 2.0 * turn_cos * turn_sin
        have *= 2
    return cos_rows, sin_rows


def gather_kernel(offset_ref, echoes_ref, gates_ref, visible_ref, pulses_ref, shown_ref, send_sub, recv_sub, send_vis, recv_vis, send_tile, recv_tile):
    sub_count, tile_count = lax.axis_size("sub"), lax.axis_size("tile")
    sub, tile = lax.axis_index("sub"), lax.axis_index("tile")
    half_dev, pulse_dev, freqs = gates_ref.shape
    subs = [lax.rem(sub + k, sub_count) for k in range(1, sub_count)]
    tiles = [lax.rem(tile + k, tile_count) for k in range(1, tile_count)]

    barrier = pltpu.get_barrier_semaphore()
    for other in subs:
        pl.semaphore_signal(barrier, inc=1, device_id=(other, tile), device_id_type=MESH)
    for other in tiles:
        pl.semaphore_signal(barrier, inc=1, device_id=(sub, other), device_id_type=MESH)

    half_total = half_dev * sub_count
    for slot in range(half_dev):
        number = (sub * half_dev + slot).astype(jnp.float32)
        angle = jnp.concatenate(
            [jnp.full((1, freqs), two_pi * (number + offset_ref[slot, p]) / half_total) for p in range(pulse_dev)], axis=1
        )
        gates = jnp.concatenate([gates_ref[slot, p : p + 1, :] for p in range(pulse_dev)], axis=1)
        wave = 0.5 + gates.astype(jnp.float32) / GATES
        cos_angle, sin_angle = sincos(angle)
        real = jnp.concatenate([echoes_ref[slot, p : p + 1, :freqs] for p in range(pulse_dev)], axis=1)
        imag = jnp.concatenate([echoes_ref[slot, p : p + 1, freqs:] for p in range(pulse_dev)], axis=1)
        rows = jnp.concatenate([real, imag, wave * cos_angle, wave * sin_angle], axis=0)
        pulses_ref[tile, sub, 4 * slot : 4 * slot + 4, :] = rows
    shown_ref[sub] = visible_ref[...]
    pl.semaphore_wait(barrier, len(subs) + len(tiles))

    first = []
    for k, other in enumerate(subs):
        for ref, send, recv in (
            (pulses_ref.at[tile, sub], send_sub, recv_sub),
            (shown_ref.at[sub], send_vis, recv_vis),
        ):
            copy = pltpu.make_async_remote_copy(
                src_ref=ref, dst_ref=ref, send_sem=send.at[k], recv_sem=recv.at[k],
                device_id=(other, tile), device_id_type=MESH,
            )
            copy.start()
            first.append(copy)
    for copy in first:
        copy.wait()
    second = []
    for k, other in enumerate(tiles):
        copy = pltpu.make_async_remote_copy(
            src_ref=pulses_ref.at[tile], dst_ref=pulses_ref.at[tile], send_sem=send_tile.at[k], recv_sem=recv_tile.at[k],
            device_id=(sub, other), device_id_type=MESH,
        )
        copy.start()
        second.append(copy)
    for copy in second:
        copy.wait()


def image_kernel(sizes, shown_ref, pulses_ref, images_ref, peak_ref, left_ref, right_ref, acc_ref, prev_ref, own_first, own_prev):
    half_dev, sub_count, tile_count, tile_dev, own_rows, block = sizes
    half_total = half_dev * sub_count
    step = pl.program_id(0)
    sub = lax.axis_index("sub")
    first_tile = lax.axis_index("tile") * tile_dev
    half = lax.rem(sub * half_dev + step, half_total)
    source = lax.div(half, half_dev)
    slot = lax.rem(half, half_dev)
    own_start = sub * own_rows
    norm_scale = (2.0 * PULSE_H * FREQS) ** (-0.5)

    def accumulate(rows, start):
        total = rows * tile_dev

        def chunk(d, carry):
            echo_real, echo_imag, cosine_wave, sine_wave = (
                pulses_ref[d, source, pl.ds(4 * slot + row, 1), :] for row in range(4)
            )
            right_cos, right_sin = powers(sine_wave, 0, PIX)
            right_cos, right_sin = right_cos.astype(jnp.bfloat16), right_sin.astype(jnp.bfloat16)
            right_ref[:PIX, :block] = right_cos
            right_ref[:PIX, block:] = -right_sin
            right_ref[PIX:, :block] = right_sin
            right_ref[PIX:, block:] = right_cos
            base_cos, base_sin = powers(cosine_wave, start, rows)
            tiles = lax.broadcasted_iota(jnp.int32, (tile_dev, block), 0) + first_tile
            column = (lax.rem(tiles, grid_cols) * PIX - 8 * PIX).astype(jnp.float32)
            row_start = (lax.div(tiles, grid_cols) * PIX - 4 * PIX).astype(jnp.float32)
            offset_cos, offset_sin = sincos(cosine_wave * column + sine_wave * row_start)
            turned_real = norm_scale * (echo_real * offset_cos - echo_imag * offset_sin)
            turned_imag = norm_scale * (echo_real * offset_sin + echo_imag * offset_cos)
            pieces = []
            for i in range(tile_dev):
                real, imag = turned_real[i : i + 1], turned_imag[i : i + 1]
                left_real = real * base_cos - imag * base_sin
                left_imag = real * base_sin + imag * base_cos
                if rows % 16 == 0:
                    left_ref[i * rows : (i + 1) * rows, :block] = left_real.astype(jnp.bfloat16)
                    left_ref[i * rows : (i + 1) * rows, block:] = left_imag.astype(jnp.bfloat16)
                else:
                    pieces.append(jnp.concatenate([left_real, left_imag], axis=1))
            if pieces:
                left_ref[:total, :] = jnp.concatenate(pieces, axis=0).astype(jnp.bfloat16)
            term = lax.dot_general(
                left_ref[:total, :], right_ref[...], (((1,), (1,)), ((), ())),
                preferred_element_type=jnp.float32,
            )
            acc_ref[:total, :] += term
            return carry

        acc_ref[:total, :] = jnp.zeros((total, 2 * PIX), jnp.float32)
        lax.fori_loop(0, tile_count, chunk, 0)

    def add_power(i, own):
        power = own[:, :PIX] * own[:, :PIX] + own[:, PIX:] * own[:, PIX:]
        peak_ref[i] = jnp.maximum(peak_ref[i], power)

    @pl.when(step <= half_dev)
    def _():
        accumulate(PIX, 0)
        for i in range(tile_dev):
            shown = shown_ref[source, slot, i].astype(jnp.float32)
            acc_ref[i * PIX : (i + 1) * PIX, :] = acc_ref[i * PIX : (i + 1) * PIX, :] * shown

        @pl.when(step == 0)
        def _():
            peak_ref[...] = jnp.zeros_like(peak_ref)
            for i in range(tile_dev):
                own_first[i] = acc_ref[pl.ds(pl.multiple_of(own_start + i * PIX, 8), own_rows), :]

        for i in range(tile_dev):
            own = acc_ref[pl.ds(pl.multiple_of(own_start + i * PIX, 8), own_rows), :]

            @pl.when(step > 0)
            def _():
                images_ref[0, i] = prev_ref[i * PIX : (i + 1) * PIX, :] + acc_ref[i * PIX : (i + 1) * PIX, :]
                add_power(i, own_prev[i] + own)

            prev_ref[i * PIX : (i + 1) * PIX, :] = acc_ref[i * PIX : (i + 1) * PIX, :]
            own_prev[i] = own

    @pl.when(step > half_dev)
    def _():
        accumulate(own_rows, own_start)
        for i in range(tile_dev):
            shown = shown_ref[source, slot, i].astype(jnp.float32)
            own = acc_ref[i * own_rows : (i + 1) * own_rows, :] * shown
            add_power(i, own_prev[i] + own)
            own_prev[i] = own

    @pl.when(step == half_total - 1)
    def _():
        for i in range(tile_dev):
            if half_total > half_dev:
                add_power(i, own_prev[i] + own_first[i])


def on_device(echoes, pulse_offset, range_gates, visible):
    half_dev, pulse_dev, _ = echoes.shape
    tile_dev = visible.shape[1]
    sub_count = lax.axis_size("sub")
    tile_count = lax.axis_size("tile")
    half_total = half_dev * sub_count
    own_rows = PIX // sub_count
    block = pulse_dev * FREQS
    vmem = pl.BlockSpec(memory_space=pltpu.VMEM)
    pulses, shown = pl.pallas_call(
        gather_kernel,
        out_shape=(
            jax.ShapeDtypeStruct((tile_count, sub_count, half_dev * 4, block), jnp.float32),
            jax.ShapeDtypeStruct((sub_count, half_dev, tile_dev), jnp.int32),
        ),
        in_specs=[pl.BlockSpec(memory_space=pltpu.SMEM), vmem, vmem, vmem],
        out_specs=(vmem, vmem),
        scratch_shapes=[pltpu.SemaphoreType.DMA((sub_count - 1,))] * 4 + [pltpu.SemaphoreType.DMA((tile_count - 1,))] * 2,
        compiler_params=pltpu.CompilerParams(collective_id=0, has_side_effects=True),
    )(pulse_offset, echoes, range_gates, visible)
    sizes = (half_dev, sub_count, tile_count, tile_dev, own_rows, block)
    images, peak = pl.pallas_call(
        functools.partial(image_kernel, sizes),
        grid=(half_total,),
        out_shape=(
            jax.ShapeDtypeStruct((half_dev, tile_dev, PIX, 2 * PIX), jnp.float32),
            jax.ShapeDtypeStruct((tile_dev, own_rows, PIX), jnp.float32),
        ),
        in_specs=[
            pl.BlockSpec(memory_space=pltpu.SMEM),
            vmem,
        ],
        out_specs=(
            pl.BlockSpec((1, tile_dev, PIX, 2 * PIX), lambda j: (jnp.clip(j - 1, 0, half_dev - 1), 0, 0, 0)),
            pl.BlockSpec((tile_dev, own_rows, PIX), lambda j: (0, 0, 0)),
        ),
        scratch_shapes=[
            pltpu.VMEM((tile_dev * PIX, 2 * block), jnp.bfloat16),
            pltpu.VMEM((2 * PIX, 2 * block), jnp.bfloat16),
            pltpu.VMEM((tile_dev * PIX, 2 * PIX), jnp.float32),
            pltpu.VMEM((tile_dev * PIX, 2 * PIX), jnp.float32),
            pltpu.VMEM((tile_dev, own_rows, 2 * PIX), jnp.float32),
            pltpu.VMEM((tile_dev, own_rows, 2 * PIX), jnp.float32),
        ],
        compiler_params=pltpu.CompilerParams(vmem_limit_bytes=40 * 2**20),
    )(shown, pulses)
    return images, peak


def solution(mesh):
    in_specs = (P("sub", "tile", None), P("sub", "tile"), P("sub", "tile", None), P("sub", "tile"))
    out_specs = (P("sub", "tile", None, None), P("tile", "sub", None))
    return jax.shard_map(
        on_device, mesh=mesh, in_specs=in_specs, out_specs=out_specs, check_vma=False
    )
```

```python
import functools
import math

import jax
import jax.numpy as jnp
from jax import lax
from jax.experimental import pallas as pl
from jax.experimental.pallas import tpu as pltpu
from jax.sharding import PartitionSpec as P

PULSE_H = 32
FREQS = 64
PIX = 128
GATES = 512

grid_cols = 16
two_pi = 2.0 * math.pi
MESH = pl.DeviceIdType.MESH

HALF_PI_A = 1.5703125
HALF_PI_B = 4.837512969970703e-4
HALF_PI_C = 7.549789948768648e-8


def sincos(phase):
    turns = jnp.floor(phase * (2.0 / math.pi) + 0.5)
    rest = phase - turns * HALF_PI_A
    rest = rest - turns * HALF_PI_B
    rest = rest - turns * HALF_PI_C
    quadrant = turns.astype(jnp.int32)
    square = rest * rest
    sine = -1.9515295891e-4 * square + 8.3321608736e-3
    sine = sine * square - 1.6666654611e-1
    sine = sine * square * rest + rest
    cosine = 2.443315711809948e-5 * square - 1.388731625493765e-3
    cosine = cosine * square + 4.166664568298827e-2
    cosine = cosine * square * square - 0.5 * square + 1.0
    odd = (quadrant & 1) == 1
    cos_out = jnp.where(odd, sine, cosine)
    sin_out = jnp.where(odd, cosine, sine)
    cos_out = jnp.where(((quadrant + 1) & 2) == 2, -cos_out, cos_out)
    sin_out = jnp.where((quadrant & 2) == 2, -sin_out, sin_out)
    return cos_out, sin_out


def walk(cos_rows, sin_rows, turn_cos, turn_sin, count):
    blocks = [(cos_rows, sin_rows)]
    if count > 1:
        blocks.append((cos_rows * turn_cos - sin_rows * turn_sin, cos_rows * turn_sin + sin_rows * turn_cos))
    double = 2.0 * turn_cos
    for _ in range(count - 2):
        (old_cos, old_sin), (now_cos, now_sin) = blocks[-2:]
        blocks.append((double * now_cos - old_cos, double * now_sin - old_sin))
    return blocks


def gather_kernel(offset_ref, echoes_ref, gates_ref, visible_ref, pulses_ref, shown_ref, send_sub, recv_sub, send_vis, recv_vis, send_tile, recv_tile):
    sub_count, tile_count = lax.axis_size("sub"), lax.axis_size("tile")
    sub, tile = lax.axis_index("sub"), lax.axis_index("tile")
    half_dev, pulse_dev, freqs = gates_ref.shape
    subs = [lax.rem(sub + k, sub_count) for k in range(1, sub_count)]
    tiles = [lax.rem(tile + k, tile_count) for k in range(1, tile_count)]

    barrier = pltpu.get_barrier_semaphore()
    for other in subs:
        pl.semaphore_signal(barrier, inc=1, device_id=(other, tile), device_id_type=MESH)
    for other in tiles:
        pl.semaphore_signal(barrier, inc=1, device_id=(sub, other), device_id_type=MESH)

    half_total = half_dev * sub_count
    for slot in range(half_dev):
        number = (sub * half_dev + slot).astype(jnp.float32)
        angle = jnp.concatenate(
            [jnp.full((1, freqs), two_pi * (number + offset_ref[slot, p]) / half_total) for p in range(pulse_dev)], axis=1
        )
        gates = jnp.concatenate([gates_ref[slot, p : p + 1, :] for p in range(pulse_dev)], axis=1)
        wave = 0.5 + gates.astype(jnp.float32) / GATES
        cos_angle, sin_angle = sincos(angle)
        real = jnp.concatenate([echoes_ref[slot, p : p + 1, :freqs] for p in range(pulse_dev)], axis=1)
        imag = jnp.concatenate([echoes_ref[slot, p : p + 1, freqs:] for p in range(pulse_dev)], axis=1)
        rows = jnp.concatenate([real, imag, wave * cos_angle, wave * sin_angle], axis=0)
        pulses_ref[tile, sub, 4 * slot : 4 * slot + 4, :] = rows
    shown_ref[sub] = visible_ref[...]
    pl.semaphore_wait(barrier, len(subs) + len(tiles))

    first = []
    for k, other in enumerate(subs):
        for ref, send, recv in (
            (pulses_ref.at[tile, sub], send_sub, recv_sub),
            (shown_ref.at[sub], send_vis, recv_vis),
        ):
            copy = pltpu.make_async_remote_copy(
                src_ref=ref, dst_ref=ref, send_sem=send.at[k], recv_sem=recv.at[k],
                device_id=(other, tile), device_id_type=MESH,
            )
            copy.start()
            first.append(copy)
    for copy in first:
        copy.wait()
    second = []
    for k, other in enumerate(tiles):
        copy = pltpu.make_async_remote_copy(
            src_ref=pulses_ref.at[tile], dst_ref=pulses_ref.at[tile], send_sem=send_tile.at[k], recv_sem=recv_tile.at[k],
            device_id=(sub, other), device_id_type=MESH,
        )
        copy.start()
        second.append(copy)
    for copy in second:
        copy.wait()


def image_kernel(sizes, shown_ref, pulses_ref, images_ref, peak_ref, left_ref, right_ref, left_odd, right_odd, acc_ref, prev_ref, own_first, own_prev):
    half_dev, sub_count, tile_count, tile_dev, own_rows, block = sizes
    half_total = half_dev * sub_count
    step = pl.program_id(0)
    sub = lax.axis_index("sub")
    first_tile = lax.axis_index("tile") * tile_dev
    half = lax.rem(sub * half_dev + step, half_total)
    source = lax.div(half, half_dev)
    slot = lax.rem(half, half_dev)
    own_start = sub * own_rows
    shown_row = shown_ref[source, pl.ds(slot, 1), :].astype(jnp.float32)
    norm_scale = (2.0 * PULSE_H * FREQS) ** (-0.5)

    def accumulate(rows, start):
        total = rows * tile_dev
        high = min(16, rows)

        def generate(d, left_ref, right_ref):
            echo_real, echo_imag, cosine_wave, sine_wave = (
                pulses_ref[d, source, pl.ds(4 * slot + row, 1), :] for row in range(4)
            )
            steps = lax.broadcasted_iota(jnp.int32, (8, block), 0)
            turn_ca = jnp.where(steps == 0, 8, jnp.where(steps == 1, 16, jnp.where(steps == 2, PIX, 0)))
            turn_sa = jnp.where(steps == 3, 8, jnp.where(steps == 4, 16, 0))
            turn_cos, turn_sin = sincos(cosine_wave * turn_ca.astype(jnp.float32) + sine_wave * turn_sa.astype(jnp.float32))

            def turn(row):
                return turn_cos[row : row + 1], turn_sin[row : row + 1]

            right_cos, right_sin = sincos(sine_wave * steps.astype(jnp.float32))
            both = walk(right_cos, right_sin, *turn(3), 2)
            right_cos, right_sin = (jnp.concatenate(pair, axis=0) for pair in zip(*both))
            for n, (cos_rows, sin_rows) in enumerate(walk(right_cos, right_sin, *turn(4), PIX // 16)):
                cos_rows, sin_rows = cos_rows.astype(jnp.bfloat16), sin_rows.astype(jnp.bfloat16)
                right_ref[16 * n : 16 * n + 16, :block] = cos_rows
                right_ref[16 * n : 16 * n + 16, block:] = -sin_rows
                right_ref[PIX + 16 * n : PIX + 16 * n + 16, :block] = sin_rows
                right_ref[PIX + 16 * n : PIX + 16 * n + 16, block:] = cos_rows

            column = lax.rem(first_tile, grid_cols) * PIX - 8 * PIX + start
            row_start = (lax.div(first_tile, grid_cols) * PIX - 4 * PIX).astype(jnp.float32)
            left_cos, left_sin = sincos(cosine_wave * (steps + column).astype(jnp.float32) + sine_wave * row_start)
            echo_real, echo_imag = norm_scale * echo_real, norm_scale * echo_imag
            left_real = echo_real * left_cos - echo_imag * left_sin
            left_imag = echo_real * left_sin + echo_imag * left_cos
            if high == 16:
                both = walk(left_real, left_imag, *turn(0), 2)
                left_real, left_imag = (jnp.concatenate(pair, axis=0) for pair in zip(*both))
            tile_cos, tile_sin = turn(2)
            next_real = left_real * tile_cos - left_imag * tile_sin
            next_imag = left_real * tile_sin + left_imag * tile_cos
            double = 2.0 * tile_cos
            count = rows // high
            pieces = []
            for n, (now, later) in enumerate(
                zip(walk(left_real, left_imag, *turn(1), count), walk(next_real, next_imag, *turn(1), count))
            ):
                for i in range(tile_dev):
                    here = i * rows + n * high
                    if high == 16:
                        left_ref[here : here + high, :block] = now[0].astype(jnp.bfloat16)
                        left_ref[here : here + high, block:] = now[1].astype(jnp.bfloat16)
                    else:
                        pieces.append(jnp.concatenate(now, axis=1))
                    now, later = later, (double * later[0] - now[0], double * later[1] - now[1])
            if pieces:
                left_ref[:total, :] = jnp.concatenate(pieces, axis=0).astype(jnp.bfloat16)

        def multiply(left_ref, right_ref):
            acc_ref[:total, :] += lax.dot_general(
                left_ref[:total, :], right_ref[...], (((1,), (1,)), ((), ())),
                preferred_element_type=jnp.float32,
            )

        def two_chunks(pair, carry):
            generate(2 * pair + 1, *odd)
            multiply(*even)
            generate(2 * pair + 2, *even)
            multiply(*odd)
            return carry

        even, odd = (left_ref, right_ref), (left_odd, right_odd)
        acc_ref[:total, :] = jnp.zeros((total, 2 * PIX), jnp.float32)
        generate(0, *even)
        lax.fori_loop(0, tile_count // 2 - 1, two_chunks, 0)
        generate(tile_count - 1, *odd)
        multiply(*even)
        multiply(*odd)

    def add_power(i, own):
        power = own[:, :PIX] * own[:, :PIX] + own[:, PIX:] * own[:, PIX:]
        peak_ref[i] = jnp.maximum(peak_ref[i], power)

    @pl.when(step <= half_dev)
    def _():
        accumulate(PIX, 0)
        for i in range(tile_dev):
            shown = shown_row[:, i : i + 1]
            acc_ref[i * PIX : (i + 1) * PIX, :] = acc_ref[i * PIX : (i + 1) * PIX, :] * shown

        @pl.when(step == 0)
        def _():
            peak_ref[...] = jnp.zeros_like(peak_ref)
            for i in range(tile_dev):
                own_first[i] = acc_ref[pl.ds(pl.multiple_of(own_start + i * PIX, 8), own_rows), :]

        for i in range(tile_dev):
            own = acc_ref[pl.ds(pl.multiple_of(own_start + i * PIX, 8), own_rows), :]

            @pl.when(step > 0)
            def _():
                images_ref[0, i] = prev_ref[i * PIX : (i + 1) * PIX, :] + acc_ref[i * PIX : (i + 1) * PIX, :]
                add_power(i, own_prev[i] + own)

            prev_ref[i * PIX : (i + 1) * PIX, :] = acc_ref[i * PIX : (i + 1) * PIX, :]
            own_prev[i] = own

    @pl.when(step > half_dev)
    def _():
        accumulate(own_rows, own_start)
        for i in range(tile_dev):
            shown = shown_row[:, i : i + 1]
            own = acc_ref[i * own_rows : (i + 1) * own_rows, :] * shown
            add_power(i, own_prev[i] + own)
            own_prev[i] = own

    @pl.when(step == half_total - 1)
    def _():
        for i in range(tile_dev):
            if half_total > half_dev:
                add_power(i, own_prev[i] + own_first[i])


def on_device(echoes, pulse_offset, range_gates, visible):
    half_dev, pulse_dev, _ = echoes.shape
    tile_dev = visible.shape[1]
    sub_count = lax.axis_size("sub")
    tile_count = lax.axis_size("tile")
    half_total = half_dev * sub_count
    own_rows = PIX // sub_count
    block = pulse_dev * FREQS
    vmem = pl.BlockSpec(memory_space=pltpu.VMEM)
    pulses, shown = pl.pallas_call(
        gather_kernel,
        out_shape=(
            jax.ShapeDtypeStruct((tile_count, sub_count, half_dev * 4, block), jnp.float32),
            jax.ShapeDtypeStruct((sub_count, half_dev, tile_dev), jnp.int32),
        ),
        in_specs=[pl.BlockSpec(memory_space=pltpu.SMEM), vmem, vmem, vmem],
        out_specs=(vmem, vmem),
        scratch_shapes=[pltpu.SemaphoreType.DMA((sub_count - 1,))] * 4 + [pltpu.SemaphoreType.DMA((tile_count - 1,))] * 2,
        compiler_params=pltpu.CompilerParams(collective_id=0, has_side_effects=True),
    )(pulse_offset, echoes, range_gates, visible)
    sizes = (half_dev, sub_count, tile_count, tile_dev, own_rows, block)
    images, peak = pl.pallas_call(
        functools.partial(image_kernel, sizes),
        grid=(half_total,),
        out_shape=(
            jax.ShapeDtypeStruct((half_dev, tile_dev, PIX, 2 * PIX), jnp.float32),
            jax.ShapeDtypeStruct((tile_dev, own_rows, PIX), jnp.float32),
        ),
        in_specs=[
            vmem,
            vmem,
        ],
        out_specs=(
            pl.BlockSpec((1, tile_dev, PIX, 2 * PIX), lambda j: (jnp.clip(j - 1, 0, half_dev - 1), 0, 0, 0)),
            pl.BlockSpec((tile_dev, own_rows, PIX), lambda j: (0, 0, 0)),
        ),
        scratch_shapes=[
            pltpu.VMEM((tile_dev * PIX, 2 * block), jnp.bfloat16),
            pltpu.VMEM((2 * PIX, 2 * block), jnp.bfloat16),
            pltpu.VMEM((tile_dev * PIX, 2 * block), jnp.bfloat16),
            pltpu.VMEM((2 * PIX, 2 * block), jnp.bfloat16),
            pltpu.VMEM((tile_dev * PIX, 2 * PIX), jnp.float32),
            pltpu.VMEM((tile_dev * PIX, 2 * PIX), jnp.float32),
            pltpu.VMEM((tile_dev, own_rows, 2 * PIX), jnp.float32),
            pltpu.VMEM((tile_dev, own_rows, 2 * PIX), jnp.float32),
        ],
        compiler_params=pltpu.CompilerParams(vmem_limit_bytes=40 * 2**20),
    )(shown, pulses)
    return images, peak


def solution(mesh):
    in_specs = (P("sub", "tile", None), P("sub", "tile"), P("sub", "tile", None), P("sub", "tile"))
    out_specs = (P("sub", "tile", None, None), P("tile", "sub", None))
    return jax.shard_map(
        on_device, mesh=mesh, in_specs=in_specs, out_specs=out_specs, check_vma=False
    )
```

```python
import functools
import math

import jax
import jax.numpy as jnp
from jax import lax
from jax.experimental import pallas as pl
from jax.experimental.pallas import tpu as pltpu
from jax.sharding import PartitionSpec as P

PULSE_H = 32
FREQS = 64
PIX = 128
GATES = 512

grid_cols = 16
two_pi = 2.0 * math.pi
MESH = pl.DeviceIdType.MESH

HALF_PI_A = 1.5703125
HALF_PI_B = 4.837512969970703e-4
HALF_PI_C = 7.549789948768648e-8


def sincos(phase):
    turns = jnp.floor(phase * (2.0 / math.pi) + 0.5)
    rest = phase - turns * HALF_PI_A
    rest = rest - turns * HALF_PI_B
    rest = rest - turns * HALF_PI_C
    quadrant = turns.astype(jnp.int32)
    square = rest * rest
    sine = -1.9515295891e-4 * square + 8.3321608736e-3
    sine = sine * square - 1.6666654611e-1
    sine = sine * square * rest + rest
    cosine = 2.443315711809948e-5 * square - 1.388731625493765e-3
    cosine = cosine * square + 4.166664568298827e-2
    cosine = cosine * square * square - 0.5 * square + 1.0
    odd = (quadrant & 1) == 1
    cos_out = jnp.where(odd, sine, cosine)
    sin_out = jnp.where(odd, cosine, sine)
    cos_out = jnp.where(((quadrant + 1) & 2) == 2, -cos_out, cos_out)
    sin_out = jnp.where((quadrant & 2) == 2, -sin_out, sin_out)
    return cos_out, sin_out


def walk(cos_rows, sin_rows, turn_cos, turn_sin, count):
    blocks = [(cos_rows, sin_rows)]
    if count > 1:
        blocks.append((cos_rows * turn_cos - sin_rows * turn_sin, cos_rows * turn_sin + sin_rows * turn_cos))
    double = 2.0 * turn_cos
    for _ in range(count - 2):
        (old_cos, old_sin), (now_cos, now_sin) = blocks[-2:]
        blocks.append((double * now_cos - old_cos, double * now_sin - old_sin))
    return blocks


def gather_kernel(offset_ref, echoes_ref, gates_ref, visible_ref, pulses_ref, shown_ref, send_sub, recv_sub, send_vis, recv_vis, send_tile, recv_tile):
    sub_count, tile_count = lax.axis_size("sub"), lax.axis_size("tile")
    sub, tile = lax.axis_index("sub"), lax.axis_index("tile")
    half_dev, pulse_dev, freqs = gates_ref.shape
    subs = [lax.rem(sub + k, sub_count) for k in range(1, sub_count)]
    tiles = [lax.rem(tile + k, tile_count) for k in range(1, tile_count)]

    barrier = pltpu.get_barrier_semaphore()
    for other in subs:
        pl.semaphore_signal(barrier, inc=1, device_id=(other, tile), device_id_type=MESH)
    for other in tiles:
        pl.semaphore_signal(barrier, inc=1, device_id=(sub, other), device_id_type=MESH)

    half_total = half_dev * sub_count
    for slot in range(half_dev):
        number = (sub * half_dev + slot).astype(jnp.float32)
        angle = jnp.concatenate(
            [jnp.full((1, freqs), two_pi * (number + offset_ref[slot, p]) / half_total) for p in range(pulse_dev)], axis=1
        )
        gates = jnp.concatenate([gates_ref[slot, p : p + 1, :] for p in range(pulse_dev)], axis=1)
        wave = 0.5 + gates.astype(jnp.float32) / GATES
        cos_angle, sin_angle = sincos(angle)
        real = jnp.concatenate([echoes_ref[slot, p : p + 1, :freqs] for p in range(pulse_dev)], axis=1)
        imag = jnp.concatenate([echoes_ref[slot, p : p + 1, freqs:] for p in range(pulse_dev)], axis=1)
        rows = jnp.concatenate([real, imag, wave * cos_angle, wave * sin_angle], axis=0)
        pulses_ref[tile, sub, 4 * slot : 4 * slot + 4, :] = rows
    shown_ref[sub] = visible_ref[...]
    pl.semaphore_wait(barrier, len(subs) + len(tiles))

    first = []
    for k, other in enumerate(subs):
        for ref, send, recv in (
            (pulses_ref.at[tile, sub], send_sub, recv_sub),
            (shown_ref.at[sub], send_vis, recv_vis),
        ):
            copy = pltpu.make_async_remote_copy(
                src_ref=ref, dst_ref=ref, send_sem=send.at[k], recv_sem=recv.at[k],
                device_id=(other, tile), device_id_type=MESH,
            )
            copy.start()
            first.append(copy)
    for copy in first:
        copy.wait()
    second = []
    for k, other in enumerate(tiles):
        copy = pltpu.make_async_remote_copy(
            src_ref=pulses_ref.at[tile], dst_ref=pulses_ref.at[tile], send_sem=send_tile.at[k], recv_sem=recv_tile.at[k],
            device_id=(sub, other), device_id_type=MESH,
        )
        copy.start()
        second.append(copy)
    for copy in second:
        copy.wait()


def image_kernel(sizes, shown_ref, pulses_ref, images_ref, peak_ref, left_ref, right_ref, left_odd, right_odd, acc_ref, prev_ref, own_first, own_prev):
    half_dev, sub_count, tile_count, tile_dev, own_rows, block = sizes
    half_total = half_dev * sub_count
    step = pl.program_id(0)
    sub = lax.axis_index("sub")
    first_tile = lax.axis_index("tile") * tile_dev
    half = lax.rem(sub * half_dev + step, half_total)
    source = lax.div(half, half_dev)
    slot = lax.rem(half, half_dev)
    own_start = sub * own_rows
    shown_row = shown_ref[source, pl.ds(slot, 1), :].astype(jnp.float32)
    norm_scale = (2.0 * PULSE_H * FREQS) ** (-0.5)

    def generate(rows, start, number, d, left_ref, right_ref, place):
        total = rows * tile_dev
        high = min(16, rows)
        source, slot = lax.div(number, half_dev), lax.rem(number, half_dev)
        front, back = slice(place, place + block), slice(place + block, place + 2 * block)
        echo_real, echo_imag, cosine_wave, sine_wave = (
            pulses_ref[d, source, pl.ds(4 * slot + row, 1), :] for row in range(4)
        )
        steps = lax.broadcasted_iota(jnp.int32, (8, block), 0)
        turn_ca = jnp.where(steps == 0, 8, jnp.where(steps == 1, 16, jnp.where(steps == 2, PIX, 0)))
        turn_sa = jnp.where(steps == 3, 8, jnp.where(steps == 4, 16, 0))
        turn_cos, turn_sin = sincos(cosine_wave * turn_ca.astype(jnp.float32) + sine_wave * turn_sa.astype(jnp.float32))

        def turn(row):
            return turn_cos[row : row + 1], turn_sin[row : row + 1]

        right_cos, right_sin = sincos(sine_wave * steps.astype(jnp.float32))
        both = walk(right_cos, right_sin, *turn(3), 2)
        right_cos, right_sin = (jnp.concatenate(pair, axis=0) for pair in zip(*both))
        for n, (cos_rows, sin_rows) in enumerate(walk(right_cos, right_sin, *turn(4), PIX // 16)):
            cos_rows, sin_rows = cos_rows.astype(jnp.bfloat16), sin_rows.astype(jnp.bfloat16)
            right_ref[16 * n : 16 * n + 16, front] = cos_rows
            right_ref[16 * n : 16 * n + 16, back] = -sin_rows
            right_ref[PIX + 16 * n : PIX + 16 * n + 16, front] = sin_rows
            right_ref[PIX + 16 * n : PIX + 16 * n + 16, back] = cos_rows

        column = lax.rem(first_tile, grid_cols) * PIX - 8 * PIX + start
        row_start = (lax.div(first_tile, grid_cols) * PIX - 4 * PIX).astype(jnp.float32)
        left_cos, left_sin = sincos(cosine_wave * (steps + column).astype(jnp.float32) + sine_wave * row_start)
        echo_real, echo_imag = norm_scale * echo_real, norm_scale * echo_imag
        left_real = echo_real * left_cos - echo_imag * left_sin
        left_imag = echo_real * left_sin + echo_imag * left_cos
        if high == 16:
            both = walk(left_real, left_imag, *turn(0), 2)
            left_real, left_imag = (jnp.concatenate(pair, axis=0) for pair in zip(*both))
        tile_cos, tile_sin = turn(2)
        next_real = left_real * tile_cos - left_imag * tile_sin
        next_imag = left_real * tile_sin + left_imag * tile_cos
        double = 2.0 * tile_cos
        count = rows // high
        pieces = []
        for n, (now, later) in enumerate(
            zip(walk(left_real, left_imag, *turn(1), count), walk(next_real, next_imag, *turn(1), count))
        ):
            for i in range(tile_dev):
                here = i * rows + n * high
                if high == 16:
                    left_ref[here : here + high, front] = now[0].astype(jnp.bfloat16)
                    left_ref[here : here + high, back] = now[1].astype(jnp.bfloat16)
                else:
                    pieces.append(jnp.concatenate(now, axis=1))
                now, later = later, (double * later[0] - now[0], double * later[1] - now[1])
        if pieces:
            left_ref[:total, place : place + 2 * block] = jnp.concatenate(pieces, axis=0).astype(jnp.bfloat16)

    def generate_group(rows, start, number, group, refs):
        for c in range(2):
            generate(rows, start, number, 2 * group + c, *refs, 2 * block * c)

    def multiply(rows, left_ref, right_ref, fresh=False):
        total = rows * tile_dev
        term = lax.dot_general(
            left_ref[:total, :], right_ref[...], (((1,), (1,)), ((), ())),
            preferred_element_type=jnp.float32,
        )
        acc_ref[:total, :] = term if fresh else acc_ref[:total, :] + term

    groups = tile_count // 2
    following = lax.rem(half + 1, half_total)
    even, odd = (left_ref, right_ref), (left_odd, right_odd)

    def accumulate(rows, start):
        generate_group(rows, start, half, 1, odd)
        multiply(rows, *even, fresh=True)

        def two_groups(pair, carry):
            generate_group(rows, start, half, 2 * pair, even)
            multiply(rows, *odd)
            generate_group(rows, start, half, 2 * pair + 1, odd)
            multiply(rows, *even)
            return carry

        lax.fori_loop(1, groups // 2, two_groups, 0)

    def add_power(i, own):
        power = own[:, :PIX] * own[:, :PIX] + own[:, PIX:] * own[:, PIX:]
        peak_ref[i] = jnp.maximum(peak_ref[i], power)

    @pl.when(step <= half_dev)
    def _():
        @pl.when(step == 0)
        def _():
            generate_group(PIX, 0, half, 0, even)

        accumulate(PIX, 0)

        @pl.when(step < half_dev)
        def _():
            generate_group(PIX, 0, following, 0, even)
            multiply(PIX, *odd)

        @pl.when(step == half_dev)
        def _():
            generate_group(own_rows, own_start, following, 0, even)
            multiply(PIX, *odd)

        for i in range(tile_dev):
            shown = shown_row[:, i : i + 1]
            acc_ref[i * PIX : (i + 1) * PIX, :] = acc_ref[i * PIX : (i + 1) * PIX, :] * shown

        @pl.when(step == 0)
        def _():
            peak_ref[...] = jnp.zeros_like(peak_ref)
            for i in range(tile_dev):
                own_first[i] = acc_ref[pl.ds(pl.multiple_of(own_start + i * PIX, 8), own_rows), :]

        for i in range(tile_dev):
            own = acc_ref[pl.ds(pl.multiple_of(own_start + i * PIX, 8), own_rows), :]

            @pl.when(step > 0)
            def _():
                images_ref[0, i] = prev_ref[i * PIX : (i + 1) * PIX, :] + acc_ref[i * PIX : (i + 1) * PIX, :]
                add_power(i, own_prev[i] + own)

            prev_ref[i * PIX : (i + 1) * PIX, :] = acc_ref[i * PIX : (i + 1) * PIX, :]
            own_prev[i] = own

    @pl.when(step > half_dev)
    def _():
        accumulate(own_rows, own_start)
        generate_group(own_rows, own_start, following, 0, even)
        multiply(own_rows, *odd)
        for i in range(tile_dev):
            shown = shown_row[:, i : i + 1]
            own = acc_ref[i * own_rows : (i + 1) * own_rows, :] * shown
            add_power(i, own_prev[i] + own)
            own_prev[i] = own

    @pl.when(step == half_total - 1)
    def _():
        for i in range(tile_dev):
            if half_total > half_dev:
                add_power(i, own_prev[i] + own_first[i])


def on_device(echoes, pulse_offset, range_gates, visible):
    half_dev, pulse_dev, _ = echoes.shape
    tile_dev = visible.shape[1]
    sub_count = lax.axis_size("sub")
    tile_count = lax.axis_size("tile")
    half_total = half_dev * sub_count
    own_rows = PIX // sub_count
    block = pulse_dev * FREQS
    vmem = pl.BlockSpec(memory_space=pltpu.VMEM)
    pulses, shown = pl.pallas_call(
        gather_kernel,
        out_shape=(
            jax.ShapeDtypeStruct((tile_count, sub_count, half_dev * 4, block), jnp.float32),
            jax.ShapeDtypeStruct((sub_count, half_dev, tile_dev), jnp.int32),
        ),
        in_specs=[pl.BlockSpec(memory_space=pltpu.SMEM), vmem, vmem, vmem],
        out_specs=(vmem, vmem),
        scratch_shapes=[pltpu.SemaphoreType.DMA((sub_count - 1,))] * 4 + [pltpu.SemaphoreType.DMA((tile_count - 1,))] * 2,
        compiler_params=pltpu.CompilerParams(collective_id=0, has_side_effects=True),
    )(pulse_offset, echoes, range_gates, visible)
    sizes = (half_dev, sub_count, tile_count, tile_dev, own_rows, block)
    images, peak = pl.pallas_call(
        functools.partial(image_kernel, sizes),
        grid=(half_total,),
        out_shape=(
            jax.ShapeDtypeStruct((half_dev, tile_dev, PIX, 2 * PIX), jnp.float32),
            jax.ShapeDtypeStruct((tile_dev, own_rows, PIX), jnp.float32),
        ),
        in_specs=[
            vmem,
            vmem,
        ],
        out_specs=(
            pl.BlockSpec((1, tile_dev, PIX, 2 * PIX), lambda j: (jnp.clip(j - 1, 0, half_dev - 1), 0, 0, 0)),
            pl.BlockSpec((tile_dev, own_rows, PIX), lambda j: (0, 0, 0)),
        ),
        scratch_shapes=[
            pltpu.VMEM((tile_dev * PIX, 4 * block), jnp.bfloat16),
            pltpu.VMEM((2 * PIX, 4 * block), jnp.bfloat16),
            pltpu.VMEM((tile_dev * PIX, 4 * block), jnp.bfloat16),
            pltpu.VMEM((2 * PIX, 4 * block), jnp.bfloat16),
            pltpu.VMEM((tile_dev * PIX, 2 * PIX), jnp.float32),
            pltpu.VMEM((tile_dev * PIX, 2 * PIX), jnp.float32),
            pltpu.VMEM((tile_dev, own_rows, 2 * PIX), jnp.float32),
            pltpu.VMEM((tile_dev, own_rows, 2 * PIX), jnp.float32),
        ],
        compiler_params=pltpu.CompilerParams(vmem_limit_bytes=40 * 2**20),
    )(shown, pulses)
    return images, peak


def solution(mesh):
    in_specs = (P("sub", "tile", None), P("sub", "tile"), P("sub", "tile", None), P("sub", "tile"))
    out_specs = (P("sub", "tile", None, None), P("tile", "sub", None))
    return jax.shard_map(
        on_device, mesh=mesh, in_specs=in_specs, out_specs=out_specs, check_vma=False
    )
```

```python
import functools
import math

import jax
import jax.numpy as jnp
from jax import lax
from jax.experimental import pallas as pl
from jax.experimental.pallas import tpu as pltpu
from jax.sharding import PartitionSpec as P

PULSE_H = 32
FREQS = 64
PIX = 128
GATES = 512

grid_cols = 16
two_pi = 2.0 * math.pi
MESH = pl.DeviceIdType.MESH

HALF_PI_A = 1.5703125
HALF_PI_B = 4.837512969970703e-4
HALF_PI_C = 7.549789948768648e-8


def sincos(phase):
    turns = jnp.floor(phase * (2.0 / math.pi) + 0.5)
    rest = phase - turns * HALF_PI_A
    rest = rest - turns * HALF_PI_B
    rest = rest - turns * HALF_PI_C
    quadrant = turns.astype(jnp.int32)
    square = rest * rest
    sine = -1.9515295891e-4 * square + 8.3321608736e-3
    sine = sine * square - 1.6666654611e-1
    sine = sine * square * rest + rest
    cosine = 2.443315711809948e-5 * square - 1.388731625493765e-3
    cosine = cosine * square + 4.166664568298827e-2
    cosine = cosine * square * square - 0.5 * square + 1.0
    odd = (quadrant & 1) == 1
    cos_out = jnp.where(odd, sine, cosine)
    sin_out = jnp.where(odd, cosine, sine)
    cos_out = jnp.where(((quadrant + 1) & 2) == 2, -cos_out, cos_out)
    sin_out = jnp.where((quadrant & 2) == 2, -sin_out, sin_out)
    return cos_out, sin_out


def walk(cos_rows, sin_rows, turn_cos, turn_sin, count):
    blocks = [(cos_rows, sin_rows)]
    if count > 1:
        blocks.append((cos_rows * turn_cos - sin_rows * turn_sin, cos_rows * turn_sin + sin_rows * turn_cos))
    double = 2.0 * turn_cos
    for _ in range(count - 2):
        (old_cos, old_sin), (now_cos, now_sin) = blocks[-2:]
        blocks.append((double * now_cos - old_cos, double * now_sin - old_sin))
    return blocks


def gather_kernel(offset_ref, echoes_ref, gates_ref, visible_ref, pulses_ref, shown_ref, send_sub, recv_sub, send_vis, recv_vis, send_tile, recv_tile):
    sub_count, tile_count = lax.axis_size("sub"), lax.axis_size("tile")
    sub, tile = lax.axis_index("sub"), lax.axis_index("tile")
    half_dev, pulse_dev, freqs = gates_ref.shape
    subs = [lax.rem(sub + k, sub_count) for k in range(1, sub_count)]
    tiles = [lax.rem(tile + k, tile_count) for k in range(1, tile_count)]

    barrier = pltpu.get_barrier_semaphore()
    for other in subs:
        pl.semaphore_signal(barrier, inc=1, device_id=(other, tile), device_id_type=MESH)
    for other in tiles:
        pl.semaphore_signal(barrier, inc=1, device_id=(sub, other), device_id_type=MESH)

    half_total = half_dev * sub_count
    for slot in range(half_dev):
        number = (sub * half_dev + slot).astype(jnp.float32)
        angle = jnp.concatenate(
            [jnp.full((1, freqs), two_pi * (number + offset_ref[slot, p]) / half_total) for p in range(pulse_dev)], axis=1
        )
        gates = jnp.concatenate([gates_ref[slot, p : p + 1, :] for p in range(pulse_dev)], axis=1)
        wave = 0.5 + gates.astype(jnp.float32) / GATES
        cos_angle, sin_angle = sincos(angle)
        real = jnp.concatenate([echoes_ref[slot, p : p + 1, :freqs] for p in range(pulse_dev)], axis=1)
        imag = jnp.concatenate([echoes_ref[slot, p : p + 1, freqs:] for p in range(pulse_dev)], axis=1)
        rows = jnp.concatenate([real, imag, wave * cos_angle, wave * sin_angle], axis=0)
        pulses_ref[tile, sub, 4 * slot : 4 * slot + 4, :] = rows
    shown_ref[sub] = visible_ref[...]
    pl.semaphore_wait(barrier, len(subs) + len(tiles))

    first = []
    for k, other in enumerate(subs):
        for ref, send, recv in (
            (pulses_ref.at[tile, sub], send_sub, recv_sub),
            (shown_ref.at[sub], send_vis, recv_vis),
        ):
            copy = pltpu.make_async_remote_copy(
                src_ref=ref, dst_ref=ref, send_sem=send.at[k], recv_sem=recv.at[k],
                device_id=(other, tile), device_id_type=MESH,
            )
            copy.start()
            first.append(copy)
    for copy in first:
        copy.wait()
    second = []
    for k, other in enumerate(tiles):
        copy = pltpu.make_async_remote_copy(
            src_ref=pulses_ref.at[tile], dst_ref=pulses_ref.at[tile], send_sem=send_tile.at[k], recv_sem=recv_tile.at[k],
            device_id=(sub, other), device_id_type=MESH,
        )
        copy.start()
        second.append(copy)
    for copy in second:
        copy.wait()


def image_kernel(sizes, shown_ref, pulses_ref, images_ref, peak_ref, left_ref, right_ref, left_odd, right_odd, acc_ref, prev_ref, own_first, own_prev):
    half_dev, sub_count, tile_count, tile_dev, own_rows, block = sizes
    half_total = half_dev * sub_count
    step = pl.program_id(0)
    sub = lax.axis_index("sub")
    first_tile = lax.axis_index("tile") * tile_dev
    half = lax.rem(sub * half_dev + step, half_total)
    source = lax.div(half, half_dev)
    slot = lax.rem(half, half_dev)
    own_start = sub * own_rows
    shown_row = shown_ref[source, pl.ds(slot, 1), :].astype(jnp.float32)
    norm_scale = (2.0 * PULSE_H * FREQS) ** (-0.5)

    def generate(rows, start, number, d, left_ref, right_ref, place):
        total = rows * tile_dev
        high = min(16, rows)
        source, slot = lax.div(number, half_dev), lax.rem(number, half_dev)
        front, back = slice(place, place + block), slice(place + block, place + 2 * block)
        echo_real, echo_imag, cosine_wave, sine_wave = (
            pulses_ref[d, source, pl.ds(4 * slot + row, 1), :] for row in range(4)
        )
        steps = lax.broadcasted_iota(jnp.int32, (8, block), 0)
        turn_ca = jnp.where(steps == 0, 8, jnp.where(steps == 1, 16, jnp.where(steps == 2, PIX, 0)))
        turn_sa = jnp.where(steps == 3, 8, jnp.where(steps == 4, 16, 0))
        turn_cos, turn_sin = sincos(cosine_wave * turn_ca.astype(jnp.float32) + sine_wave * turn_sa.astype(jnp.float32))

        def turn(row):
            return turn_cos[row : row + 1], turn_sin[row : row + 1]

        right_cos, right_sin = sincos(sine_wave * steps.astype(jnp.float32))
        both = walk(right_cos, right_sin, *turn(3), 2)
        right_cos, right_sin = (jnp.concatenate(pair, axis=0) for pair in zip(*both))
        for n, (cos_rows, sin_rows) in enumerate(walk(right_cos, right_sin, *turn(4), PIX // 16)):
            cos_rows, sin_rows = cos_rows.astype(jnp.bfloat16), sin_rows.astype(jnp.bfloat16)
            right_ref[16 * n : 16 * n + 16, front] = cos_rows
            right_ref[16 * n : 16 * n + 16, back] = -sin_rows
            right_ref[PIX + 16 * n : PIX + 16 * n + 16, front] = sin_rows
            right_ref[PIX + 16 * n : PIX + 16 * n + 16, back] = cos_rows

        column = lax.rem(first_tile, grid_cols) * PIX - 8 * PIX + start
        row_start = (lax.div(first_tile, grid_cols) * PIX - 4 * PIX).astype(jnp.float32)
        left_cos, left_sin = sincos(cosine_wave * (steps + column).astype(jnp.float32) + sine_wave * row_start)
        echo_real, echo_imag = norm_scale * echo_real, norm_scale * echo_imag
        left_real = echo_real * left_cos - echo_imag * left_sin
        left_imag = echo_real * left_sin + echo_imag * left_cos
        if high == 16:
            both = walk(left_real, left_imag, *turn(0), 2)
            left_real, left_imag = (jnp.concatenate(pair, axis=0) for pair in zip(*both))
        tile_cos, tile_sin = turn(2)
        next_real = left_real * tile_cos - left_imag * tile_sin
        next_imag = left_real * tile_sin + left_imag * tile_cos
        double = 2.0 * tile_cos
        count = rows // high
        pieces = []
        for n, (now, later) in enumerate(
            zip(walk(left_real, left_imag, *turn(1), count), walk(next_real, next_imag, *turn(1), count))
        ):
            for i in range(tile_dev):
                here = i * rows + n * high
                if high == 16:
                    left_ref[here : here + high, front] = now[0].astype(jnp.bfloat16)
                    left_ref[here : here + high, back] = now[1].astype(jnp.bfloat16)
                else:
                    pieces.append(jnp.concatenate(now, axis=1))
                now, later = later, (double * later[0] - now[0], double * later[1] - now[1])
        if pieces:
            left_ref[:total, place : place + 2 * block] = jnp.concatenate(pieces, axis=0).astype(jnp.bfloat16)

    def generate_group(rows, start, number, group, refs):
        for c in range(4):
            generate(rows, start, number, 4 * group + c, *refs, 2 * block * c)

    def multiply(rows, left_ref, right_ref, fresh=False):
        total = rows * tile_dev
        term = lax.dot_general(
            left_ref[:total, :], right_ref[...], (((1,), (1,)), ((), ())),
            preferred_element_type=jnp.float32,
        )
        acc_ref[:total, :] = term if fresh else acc_ref[:total, :] + term

    groups = tile_count // 4
    following = lax.rem(half + 1, half_total)
    even, odd = (left_ref, right_ref), (left_odd, right_odd)

    def accumulate(rows, start):
        generate_group(rows, start, half, 1, odd)
        multiply(rows, *even, fresh=True)

        def two_groups(pair, carry):
            generate_group(rows, start, half, 2 * pair, even)
            multiply(rows, *odd)
            generate_group(rows, start, half, 2 * pair + 1, odd)
            multiply(rows, *even)
            return carry

        lax.fori_loop(1, groups // 2, two_groups, 0)

    def add_power(i, own):
        power = own[:, :PIX] * own[:, :PIX] + own[:, PIX:] * own[:, PIX:]
        peak_ref[i] = jnp.maximum(peak_ref[i], power)

    @pl.when(step <= half_dev)
    def _():
        @pl.when(step == 0)
        def _():
            generate_group(PIX, 0, half, 0, even)

        accumulate(PIX, 0)

        @pl.when(step < half_dev)
        def _():
            generate_group(PIX, 0, following, 0, even)
            multiply(PIX, *odd)

        @pl.when(step == half_dev)
        def _():
            generate_group(own_rows, own_start, following, 0, even)
            multiply(PIX, *odd)

        for i in range(tile_dev):
            shown = shown_row[:, i : i + 1]
            acc_ref[i * PIX : (i + 1) * PIX, :] = acc_ref[i * PIX : (i + 1) * PIX, :] * shown

        @pl.when(step == 0)
        def _():
            peak_ref[...] = jnp.zeros_like(peak_ref)
            for i in range(tile_dev):
                own_first[i] = acc_ref[pl.ds(pl.multiple_of(own_start + i * PIX, 8), own_rows), :]

        for i in range(tile_dev):
            own = acc_ref[pl.ds(pl.multiple_of(own_start + i * PIX, 8), own_rows), :]

            @pl.when(step > 0)
            def _():
                images_ref[0, i] = prev_ref[i * PIX : (i + 1) * PIX, :] + acc_ref[i * PIX : (i + 1) * PIX, :]
                add_power(i, own_prev[i] + own)

            prev_ref[i * PIX : (i + 1) * PIX, :] = acc_ref[i * PIX : (i + 1) * PIX, :]
            own_prev[i] = own

    @pl.when(step > half_dev)
    def _():
        accumulate(own_rows, own_start)
        generate_group(own_rows, own_start, following, 0, even)
        multiply(own_rows, *odd)
        for i in range(tile_dev):
            shown = shown_row[:, i : i + 1]
            own = acc_ref[i * own_rows : (i + 1) * own_rows, :] * shown
            add_power(i, own_prev[i] + own)
            own_prev[i] = own

    @pl.when(step == half_total - 1)
    def _():
        for i in range(tile_dev):
            if half_total > half_dev:
                add_power(i, own_prev[i] + own_first[i])


def on_device(echoes, pulse_offset, range_gates, visible):
    half_dev, pulse_dev, _ = echoes.shape
    tile_dev = visible.shape[1]
    sub_count = lax.axis_size("sub")
    tile_count = lax.axis_size("tile")
    half_total = half_dev * sub_count
    own_rows = PIX // sub_count
    block = pulse_dev * FREQS
    vmem = pl.BlockSpec(memory_space=pltpu.VMEM)
    pulses, shown = pl.pallas_call(
        gather_kernel,
        out_shape=(
            jax.ShapeDtypeStruct((tile_count, sub_count, half_dev * 4, block), jnp.float32),
            jax.ShapeDtypeStruct((sub_count, half_dev, tile_dev), jnp.int32),
        ),
        in_specs=[pl.BlockSpec(memory_space=pltpu.SMEM), vmem, vmem, vmem],
        out_specs=(vmem, vmem),
        scratch_shapes=[pltpu.SemaphoreType.DMA((sub_count - 1,))] * 4 + [pltpu.SemaphoreType.DMA((tile_count - 1,))] * 2,
        compiler_params=pltpu.CompilerParams(collective_id=0, has_side_effects=True),
    )(pulse_offset, echoes, range_gates, visible)
    sizes = (half_dev, sub_count, tile_count, tile_dev, own_rows, block)
    images, peak = pl.pallas_call(
        functools.partial(image_kernel, sizes),
        grid=(half_total,),
        out_shape=(
            jax.ShapeDtypeStruct((half_dev, tile_dev, PIX, 2 * PIX), jnp.float32),
            jax.ShapeDtypeStruct((tile_dev, own_rows, PIX), jnp.float32),
        ),
        in_specs=[
            vmem,
            vmem,
        ],
        out_specs=(
            pl.BlockSpec((1, tile_dev, PIX, 2 * PIX), lambda j: (jnp.clip(j - 1, 0, half_dev - 1), 0, 0, 0)),
            pl.BlockSpec((tile_dev, own_rows, PIX), lambda j: (0, 0, 0)),
        ),
        scratch_shapes=[
            pltpu.VMEM((tile_dev * PIX, 8 * block), jnp.bfloat16),
            pltpu.VMEM((2 * PIX, 8 * block), jnp.bfloat16),
            pltpu.VMEM((tile_dev * PIX, 8 * block), jnp.bfloat16),
            pltpu.VMEM((2 * PIX, 8 * block), jnp.bfloat16),
            pltpu.VMEM((tile_dev * PIX, 2 * PIX), jnp.float32),
            pltpu.VMEM((tile_dev * PIX, 2 * PIX), jnp.float32),
            pltpu.VMEM((tile_dev, own_rows, 2 * PIX), jnp.float32),
            pltpu.VMEM((tile_dev, own_rows, 2 * PIX), jnp.float32),
        ],
        compiler_params=pltpu.CompilerParams(vmem_limit_bytes=40 * 2**20),
    )(shown, pulses)
    return images, peak


def solution(mesh):
    in_specs = (P("sub", "tile", None), P("sub", "tile"), P("sub", "tile", None), P("sub", "tile"))
    out_specs = (P("sub", "tile", None, None), P("tile", "sub", None))
    return jax.shard_map(
        on_device, mesh=mesh, in_specs=in_specs, out_specs=out_specs, check_vma=False
    )
```

```python
import functools
import math

import jax
import jax.numpy as jnp
from jax import lax
from jax.experimental import pallas as pl
from jax.experimental.pallas import tpu as pltpu
from jax.sharding import PartitionSpec as P

PULSE_H = 32
FREQS = 64
PIX = 128
GATES = 512

grid_cols = 16
two_pi = 2.0 * math.pi
MESH = pl.DeviceIdType.MESH

HALF_PI_A = 1.5703125
HALF_PI_B = 4.837512969970703e-4
HALF_PI_C = 7.549789948768648e-8


def sincos(phase):
    turns = jnp.floor(phase * (2.0 / math.pi) + 0.5)
    rest = phase - turns * HALF_PI_A
    rest = rest - turns * HALF_PI_B
    rest = rest - turns * HALF_PI_C
    quadrant = turns.astype(jnp.int32)
    square = rest * rest
    sine = -1.9515295891e-4 * square + 8.3321608736e-3
    sine = sine * square - 1.6666654611e-1
    sine = sine * square * rest + rest
    cosine = 2.443315711809948e-5 * square - 1.388731625493765e-3
    cosine = cosine * square + 4.166664568298827e-2
    cosine = cosine * square * square - 0.5 * square + 1.0
    odd = (quadrant & 1) == 1
    cos_out = jnp.where(odd, sine, cosine)
    sin_out = jnp.where(odd, cosine, sine)
    cos_out = jnp.where(((quadrant + 1) & 2) == 2, -cos_out, cos_out)
    sin_out = jnp.where((quadrant & 2) == 2, -sin_out, sin_out)
    return cos_out, sin_out


def walk(cos_rows, sin_rows, turn_cos, turn_sin, count):
    blocks = [(cos_rows, sin_rows)]
    if count > 1:
        blocks.append((cos_rows * turn_cos - sin_rows * turn_sin, cos_rows * turn_sin + sin_rows * turn_cos))
    double = 2.0 * turn_cos
    for _ in range(count - 2):
        (old_cos, old_sin), (now_cos, now_sin) = blocks[-2:]
        blocks.append((double * now_cos - old_cos, double * now_sin - old_sin))
    return blocks


def gather_kernel(offset_ref, echoes_ref, gates_ref, visible_ref, pulses_ref, shown_ref, send_sub, recv_sub, send_vis, recv_vis, send_tile, recv_tile):
    sub_count, tile_count = lax.axis_size("sub"), lax.axis_size("tile")
    sub, tile = lax.axis_index("sub"), lax.axis_index("tile")
    half_dev, pulse_dev, freqs = gates_ref.shape
    subs = [lax.rem(sub + k, sub_count) for k in range(1, sub_count)]
    tiles = [lax.rem(tile + k, tile_count) for k in range(1, tile_count)]

    barrier = pltpu.get_barrier_semaphore()
    for other in subs:
        pl.semaphore_signal(barrier, inc=1, device_id=(other, tile), device_id_type=MESH)
    for other in tiles:
        pl.semaphore_signal(barrier, inc=1, device_id=(sub, other), device_id_type=MESH)

    half_total = half_dev * sub_count
    for slot in range(half_dev):
        number = (sub * half_dev + slot).astype(jnp.float32)
        angle = jnp.concatenate(
            [jnp.full((1, freqs), two_pi * (number + offset_ref[slot, p]) / half_total) for p in range(pulse_dev)], axis=1
        )
        gates = jnp.concatenate([gates_ref[slot, p : p + 1, :] for p in range(pulse_dev)], axis=1)
        wave = 0.5 + gates.astype(jnp.float32) / GATES
        cos_angle, sin_angle = sincos(angle)
        real = jnp.concatenate([echoes_ref[slot, p : p + 1, :freqs] for p in range(pulse_dev)], axis=1)
        imag = jnp.concatenate([echoes_ref[slot, p : p + 1, freqs:] for p in range(pulse_dev)], axis=1)
        rows = jnp.concatenate([real, imag, wave * cos_angle, wave * sin_angle], axis=0)
        pulses_ref[tile, sub, 4 * slot : 4 * slot + 4, :] = rows
    shown_ref[sub] = visible_ref[...]
    pl.semaphore_wait(barrier, len(subs) + len(tiles))

    first = []
    for k, other in enumerate(subs):
        for ref, send, recv in (
            (pulses_ref.at[tile, sub], send_sub, recv_sub),
            (shown_ref.at[sub], send_vis, recv_vis),
        ):
            copy = pltpu.make_async_remote_copy(
                src_ref=ref, dst_ref=ref, send_sem=send.at[k], recv_sem=recv.at[k],
                device_id=(other, tile), device_id_type=MESH,
            )
            copy.start()
            first.append(copy)
    for copy in first:
        copy.wait()
    second = []
    for k, other in enumerate(tiles):
        copy = pltpu.make_async_remote_copy(
            src_ref=pulses_ref.at[tile], dst_ref=pulses_ref.at[tile], send_sem=send_tile.at[k], recv_sem=recv_tile.at[k],
            device_id=(sub, other), device_id_type=MESH,
        )
        copy.start()
        second.append(copy)
    for copy in second:
        copy.wait()


def image_kernel(sizes, shown_ref, pulses_ref, images_ref, peak_ref, left_ref, right_ref, left_odd, right_odd, acc_ref, prev_ref, own_first, own_prev):
    half_dev, sub_count, tile_count, tile_dev, own_rows, block = sizes
    half_total = half_dev * sub_count
    step = pl.program_id(0)
    sub = lax.axis_index("sub")
    first_tile = lax.axis_index("tile") * tile_dev
    half = lax.rem(sub * half_dev + step, half_total)
    source = lax.div(half, half_dev)
    slot = lax.rem(half, half_dev)
    own_start = sub * own_rows
    shown_row = shown_ref[source, pl.ds(slot, 1), :].astype(jnp.float32)
    norm_scale = (2.0 * PULSE_H * FREQS) ** (-0.5)

    def generate(rows, start, number, d, left_ref, right_ref, place):
        total = rows * tile_dev
        high = min(16, rows)
        source, slot = lax.div(number, half_dev), lax.rem(number, half_dev)
        front, back = slice(place, place + block), slice(place + block, place + 2 * block)
        echo_real, echo_imag, cosine_wave, sine_wave = (
            pulses_ref[d, source, pl.ds(4 * slot + row, 1), :] for row in range(4)
        )
        steps = lax.broadcasted_iota(jnp.int32, (8, block), 0)
        turn_ca = jnp.where(steps == 0, 8, jnp.where(steps == 1, 16, jnp.where(steps == 2, PIX, 0)))
        turn_sa = jnp.where(steps == 3, 8, jnp.where(steps == 4, 16, 0))
        turn_cos, turn_sin = sincos(cosine_wave * turn_ca.astype(jnp.float32) + sine_wave * turn_sa.astype(jnp.float32))

        def turn(row):
            return turn_cos[row : row + 1], turn_sin[row : row + 1]

        right_cos, right_sin = sincos(sine_wave * steps.astype(jnp.float32))
        both = walk(right_cos, right_sin, *turn(3), 2)
        right_cos, right_sin = (jnp.concatenate(pair, axis=0) for pair in zip(*both))
        for n, (cos_rows, sin_rows) in enumerate(walk(right_cos, right_sin, *turn(4), PIX // 16)):
            cos_rows, sin_rows = cos_rows.astype(jnp.bfloat16), sin_rows.astype(jnp.bfloat16)
            right_ref[16 * n : 16 * n + 16, front] = cos_rows
            right_ref[16 * n : 16 * n + 16, back] = -sin_rows
            right_ref[PIX + 16 * n : PIX + 16 * n + 16, front] = sin_rows
            right_ref[PIX + 16 * n : PIX + 16 * n + 16, back] = cos_rows

        column = lax.rem(first_tile, grid_cols) * PIX - 8 * PIX + start
        row_start = (lax.div(first_tile, grid_cols) * PIX - 4 * PIX).astype(jnp.float32)
        left_cos, left_sin = sincos(cosine_wave * (steps + column).astype(jnp.float32) + sine_wave * row_start)
        echo_real, echo_imag = norm_scale * echo_real, norm_scale * echo_imag
        left_real = echo_real * left_cos - echo_imag * left_sin
        left_imag = echo_real * left_sin + echo_imag * left_cos
        if high == 16:
            both = walk(left_real, left_imag, *turn(0), 2)
            left_real, left_imag = (jnp.concatenate(pair, axis=0) for pair in zip(*both))
        tile_cos, tile_sin = turn(2)
        next_real = left_real * tile_cos - left_imag * tile_sin
        next_imag = left_real * tile_sin + left_imag * tile_cos
        double = 2.0 * tile_cos
        count = rows // high
        pieces = []
        for n, (now, later) in enumerate(
            zip(walk(left_real, left_imag, *turn(1), count), walk(next_real, next_imag, *turn(1), count))
        ):
            for i in range(tile_dev):
                here = i * rows + n * high
                if high == 16:
                    left_ref[here : here + high, front] = now[0].astype(jnp.bfloat16)
                    left_ref[here : here + high, back] = now[1].astype(jnp.bfloat16)
                else:
                    pieces.append(jnp.concatenate(now, axis=1))
                now, later = later, (double * later[0] - now[0], double * later[1] - now[1])
        if pieces:
            left_ref[:total, place : place + 2 * block] = jnp.concatenate(pieces, axis=0).astype(jnp.bfloat16)

    def generate_group(rows, start, number, group, refs):
        for c in range(2):
            generate(rows, start, number, 2 * group + c, *refs, 2 * block * c)

    def multiply(rows, left_ref, right_ref, fresh=False):
        total = rows * tile_dev
        term = lax.dot_general(
            left_ref[:total, :], right_ref[...], (((1,), (1,)), ((), ())),
            preferred_element_type=jnp.float32,
        )
        acc_ref[:total, :] = term if fresh else acc_ref[:total, :] + term

    groups = tile_count // 2
    following = lax.rem(half + 1, half_total)
    even, odd = (left_ref, right_ref), (left_odd, right_odd)

    def accumulate(rows, start):
        generate_group(rows, start, half, 1, odd)
        multiply(rows, *even, fresh=True)

        def two_groups(pair, carry):
            generate_group(rows, start, half, 2 * pair, even)
            multiply(rows, *odd)
            generate_group(rows, start, half, 2 * pair + 1, odd)
            multiply(rows, *even)
            return carry

        lax.fori_loop(1, groups // 2, two_groups, 0)

    def add_power(i, own):
        power = own[:, :PIX] * own[:, :PIX] + own[:, PIX:] * own[:, PIX:]
        peak_ref[i] = jnp.maximum(peak_ref[i], power)

    @pl.when(step <= half_dev)
    def _():
        @pl.when(step == 0)
        def _():
            generate_group(PIX, 0, half, 0, even)

        accumulate(PIX, 0)

        @pl.when(step < half_dev)
        def _():
            generate_group(PIX, 0, following, 0, even)
            multiply(PIX, *odd)

        @pl.when(step == half_dev)
        def _():
            generate_group(own_rows, own_start, following, 0, even)
            multiply(PIX, *odd)

        for i in range(tile_dev):
            shown = shown_row[:, i : i + 1]
            acc_ref[i * PIX : (i + 1) * PIX, :] = acc_ref[i * PIX : (i + 1) * PIX, :] * shown

        @pl.when(step == 0)
        def _():
            peak_ref[...] = jnp.zeros_like(peak_ref)
            for i in range(tile_dev):
                own_first[i] = acc_ref[pl.ds(pl.multiple_of(own_start + i * PIX, 8), own_rows), :]

        for i in range(tile_dev):
            own = acc_ref[pl.ds(pl.multiple_of(own_start + i * PIX, 8), own_rows), :]

            @pl.when(step > 0)
            def _():
                images_ref[0, i] = prev_ref[i * PIX : (i + 1) * PIX, :] + acc_ref[i * PIX : (i + 1) * PIX, :]
                add_power(i, own_prev[i] + own)

            prev_ref[i * PIX : (i + 1) * PIX, :] = acc_ref[i * PIX : (i + 1) * PIX, :]
            own_prev[i] = own

    @pl.when(step > half_dev)
    def _():
        accumulate(own_rows, own_start)
        generate_group(own_rows, own_start, following, 0, even)
        multiply(own_rows, *odd)
        for i in range(tile_dev):
            shown = shown_row[:, i : i + 1]
            own = acc_ref[i * own_rows : (i + 1) * own_rows, :] * shown
            add_power(i, own_prev[i] + own)
            own_prev[i] = own

    @pl.when(step == half_total - 1)
    def _():
        for i in range(tile_dev):
            if half_total > half_dev:
                add_power(i, own_prev[i] + own_first[i])


def on_device(echoes, pulse_offset, range_gates, visible):
    half_dev, pulse_dev, _ = echoes.shape
    tile_dev = visible.shape[1]
    sub_count = lax.axis_size("sub")
    tile_count = lax.axis_size("tile")
    half_total = half_dev * sub_count
    own_rows = PIX // sub_count
    block = pulse_dev * FREQS
    vmem = pl.BlockSpec(memory_space=pltpu.VMEM)
    pulses, shown = pl.pallas_call(
        gather_kernel,
        out_shape=(
            jax.ShapeDtypeStruct((tile_count, sub_count, half_dev * 4, block), jnp.float32),
            jax.ShapeDtypeStruct((sub_count, half_dev, tile_dev), jnp.int32),
        ),
        in_specs=[pl.BlockSpec(memory_space=pltpu.SMEM), vmem, vmem, vmem],
        out_specs=(vmem, vmem),
        scratch_shapes=[pltpu.SemaphoreType.DMA((sub_count - 1,))] * 4 + [pltpu.SemaphoreType.DMA((tile_count - 1,))] * 2,
        compiler_params=pltpu.CompilerParams(collective_id=0, has_side_effects=True),
    )(pulse_offset, echoes, range_gates, visible)
    sizes = (half_dev, sub_count, tile_count, tile_dev, own_rows, block)
    images, peak = pl.pallas_call(
        functools.partial(image_kernel, sizes),
        grid=(half_total,),
        out_shape=(
            jax.ShapeDtypeStruct((half_dev, tile_dev, PIX, 2 * PIX), jnp.float32),
            jax.ShapeDtypeStruct((tile_dev, own_rows, PIX), jnp.float32),
        ),
        in_specs=[
            vmem,
            vmem,
        ],
        out_specs=(
            pl.BlockSpec((1, tile_dev, PIX, 2 * PIX), lambda j: (jnp.clip(j - 1, 0, half_dev - 1), 0, 0, 0)),
            pl.BlockSpec((tile_dev, own_rows, PIX), lambda j: (0, 0, 0)),
        ),
        scratch_shapes=[
            pltpu.VMEM((tile_dev * PIX, 4 * block), jnp.bfloat16),
            pltpu.VMEM((2 * PIX, 4 * block), jnp.bfloat16),
            pltpu.VMEM((tile_dev * PIX, 4 * block), jnp.bfloat16),
            pltpu.VMEM((2 * PIX, 4 * block), jnp.bfloat16),
            pltpu.VMEM((tile_dev * PIX, 2 * PIX), jnp.float32),
            pltpu.VMEM((tile_dev * PIX, 2 * PIX), jnp.float32),
            pltpu.VMEM((tile_dev, own_rows, 2 * PIX), jnp.float32),
            pltpu.VMEM((tile_dev, own_rows, 2 * PIX), jnp.float32),
        ],
        compiler_params=pltpu.CompilerParams(vmem_limit_bytes=60 * 2**20),
    )(shown, pulses)
    return images, peak


def solution(mesh):
    in_specs = (P("sub", "tile", None), P("sub", "tile"), P("sub", "tile", None), P("sub", "tile"))
    out_specs = (P("sub", "tile", None, None), P("tile", "sub", None))
    return jax.shard_map(
        on_device, mesh=mesh, in_specs=in_specs, out_specs=out_specs, check_vma=False
    )
```
